512 devices in a mesh: off: 32 (over x_lo, z), rows: 16 (over x_hi, y, core).
Axes of the slice: x: 4 (x_hi: 2, x_lo: 2; x = x_hi * 2 + x_lo), y: 4, z: 16, core: 2. Of those that a mesh axis runs over, the one named last changes fastest.
Arguments:
- volume: bfloat16 [256, 16, 64, 480], P('off', None, 'rows'), may hold values from -6 to 6
- offset_kernels: bfloat16 [2, 9, 16, 16], replicated, may hold values from -0.75 to 0.75
- offset_biases: float32 [2, 16], replicated, may hold values from -3 to 3
- spatial_kernels: bfloat16 [2, 9, 16, 16], replicated, may hold values from -0.75 to 0.75
- spatial_biases: float32 [2, 16], replicated, may hold values from -3 to 3
Outputs:
- filtered: bfloat16 [256, 16, 64, 480], P('off', None, 'rows')
The draws below stay inside these ranges and needn't reach their ends.
All inputs are finite; a program needn't handle non-finite values.
Results may differ from the reference program's by a relative error of at most 0.0058.
Values may be sent and summed in bfloat16 or wider, within the bound.
A program may use at most 64 MiB of HBM per device.

```python
import jax
import jax.numpy as jnp
from jax import lax

U = 16
CH = 16
ROUNDS = 2
W = 480
OFFSETS = 256
H = 64


def block_levels(stream_key, extent, cuts, low, top_value):
    factor_of, own = 1.0, jax.random.fold_in(stream_key, 6)
    for dim, shards_of in cuts:
        draws = jnp.exp(jax.random.uniform(jax.random.fold_in(own, dim), (shards_of,), jnp.float32, low / len(cuts), top_value / len(cuts)))
        factor_of = factor_of * jnp.repeat(draws, extent[dim] // shards_of).reshape([-1 if axis == dim else 1 for axis in range(len(extent))])
    return factor_of


def scatter_about(key, extent, spread, most, shards=(), held_as=jnp.bfloat16):
    entries = jax.random.normal(key, extent, jnp.float32) * spread
    if len(shards) > 0:
        entries = block_levels(key, extent, shards, -0.22, 0.18) * entries
    return jnp.clip(entries, min=-most, max=most).astype(held_as)


def setup_inputs(seed: int = 0) -> dict:
    arg_keys = jax.random.split(jax.random.key(seed), 6)
    volume = scatter_about(arg_keys[0], (OFFSETS, CH, H, W), 1.0, 6.0, ((0, 32), (2, 16)))
    offset_kernels = scatter_about(arg_keys[1], (ROUNDS, 9, CH, CH), (9 * CH // 2) ** -0.5, 0.75)
    offset_biases = scatter_about(arg_keys[2], (ROUNDS, CH), 0.5, 3.0, (), jnp.float32)
    spatial_kernels = scatter_about(arg_keys[3], (ROUNDS, 9, CH, CH), (9 * CH // 2) ** -0.5, 0.75)
    spatial_biases = scatter_about(arg_keys[4], (ROUNDS, CH), 0.5, 3.0, (), jnp.float32)
    return {"volume": volume, "offset_kernels": offset_kernels, "offset_biases": offset_biases, "spatial_kernels": spatial_kernels, "spatial_biases": spatial_biases}


def offset_round(plane_set, kernel, biases):
    padded = jnp.pad(plane_set, ((1, 1), (1, 1), (0, 0), (0, 0)))
    stacked = jnp.stack([padded[a:a + U, b:b + U] for a in range(3) for b in range(3)], 0)
    summed = jnp.einsum("tkc,tuvcw->uvkw", kernel.astype(jnp.float32), stacked.astype(jnp.float32), precision=lax.Precision.HIGHEST)
    return jax.nn.relu(summed + biases[:, None]).astype(jnp.bfloat16)


def spatial_round(plane, kernel, biases):
    padded = jnp.pad(plane, ((0, 0), (1, 1), (1, 1)))
    stacked = jnp.stack([padded[:, a:a + H, b:b + W] for a in range(3) for b in range(3)], 0)
    summed = jnp.einsum("tkc,tchw->khw", kernel.astype(jnp.float32), stacked.astype(jnp.float32), precision=lax.Precision.HIGHEST)
    return jax.nn.relu(summed + biases[:, None, None]).astype(jnp.bfloat16)


def reference(volume, offset_kernels, offset_biases, spatial_kernels, spatial_biases):
    current = volume
    for round_number in range(ROUNDS):
        grid_view = current.reshape(U, U, CH, H, W)
        by_image_row = jnp.moveaxis(grid_view, 3, 0)
        kernel_one = offset_kernels[round_number]
        biases_one = offset_biases[round_number]
        mixed = lax.map(lambda row_set: offset_round(row_set, kernel_one, biases_one), by_image_row)
        current = jnp.moveaxis(mixed, 0, 3).reshape(OFFSETS, CH, H, W)
        kernel_two = spatial_kernels[round_number]
        biases_two = spatial_biases[round_number]
        current = lax.map(lambda plane: spatial_round(plane, kernel_two, biases_two), current)
    return current
```

```python
import jax
import jax.numpy as jnp
from jax import lax
from jax.experimental import pallas as pl
from jax.experimental.pallas import tpu as pltpu
from jax.sharding import PartitionSpec as P

MESH = pl.DeviceIdType.MESH
CH = 16
ROUNDS = 2
HALF = 8
BLOCK = HALF * CH
ROWS = 4
WIDTH = 480
LANES = 512
OWN = BLOCK
EDGE = 3 * BLOCK
DEPTH = 512
ORDER = (0, 3, 1, 2)


def kernel(n_off, n_rows, x_ref, ok_ref, ob_ref, sk_ref, sb_ref, o_ref,
           xb, mixed, w_off, w_sp, bias, ss, rs, hs, hr):
    i, r = lax.axis_index("off"), lax.axis_index("rows")
    odd = lax.rem(i, 2)
    s = 1 - 2 * odd

    def inside(t):
        return (t >= 0) & (t < n_off)

    def row_inside(t):
        return (t >= 0) & (t < n_rows)

    barrier = pltpu.get_barrier_semaphore()
    count = jnp.int32(0)
    offs = (i - 2, i + 2, i + s, i - s, i + 3 * s)
    for t in offs:
        @pl.when(inside(t))
        def _():
            pl.semaphore_signal(barrier, inc=1, device_id=(t, r), device_id_type=MESH)
        count = count + inside(t).astype(jnp.int32)
    for t in (r - 1, r + 1):
        @pl.when(row_inside(t))
        def _():
            pl.semaphore_signal(barrier, inc=1, device_id=(i, t), device_id_type=MESH)
        count = count + row_inside(t).astype(jnp.int32)
    pl.semaphore_wait(barrier, count)

    edge_src = pl.multiple_of(OWN + (HALF - 1) * CH * (1 - odd), CH)
    near = pl.multiple_of(EDGE + 2 * CH * (1 - odd), CH)
    far = pl.multiple_of(EDGE + 2 * CH * odd, CH)

    def flows(rnd, y):
        own = pl.ds(OWN, BLOCK)
        edge = pl.ds(edge_src, CH)
        table = (
            (own, pl.ds(0, BLOCK), i + 2, i - 2),
            (own, pl.ds(2 * BLOCK, BLOCK), i - 2, i + 2),
            (edge, pl.ds(EDGE + CH, CH), i + s, i + s),
            (edge, pl.ds(near, CH), i - s, i - s),
            (edge, pl.ds(far, CH), i + 3 * s, i + 3 * s),
        )
        for f, (src, dst, to, come) in enumerate(table):
            copy = pltpu.make_async_remote_copy(
                src_ref=xb.at[rnd, y, src, :], dst_ref=xb.at[rnd, y, dst, :],
                send_sem=ss.at[rnd, y, f], recv_sem=rs.at[rnd, y, f],
                device_id=(to, r), device_id_type=MESH)
            yield copy, inside(to), inside(come)

    def send(rnd, y):
        for copy, to, _ in flows(rnd, y):
            @pl.when(to)
            def _():
                copy.start()

    def receive(rnd, y):
        for copy, _, come in flows(rnd, y):
            @pl.when(come)
            def _():
                copy.wait_recv()

    def sent(rnd, y):
        for copy, to, _ in flows(rnd, y):
            @pl.when(to)
            def _():
                copy.wait_send()

    def halo(rnd, side):
        src, dst, to, come = ((1, ROWS + 1, r - 1, r + 1), (ROWS, 0, r + 1, r - 1))[side]
        copy = pltpu.make_async_remote_copy(
            src_ref=mixed.at[rnd, pl.ds(src * BLOCK, BLOCK), :],
            dst_ref=mixed.at[rnd, pl.ds(dst * BLOCK, BLOCK), :],
            send_sem=hs.at[rnd, side], recv_sem=hr.at[rnd, side],
            device_id=(i, to), device_id_type=MESH)
        return copy, row_inside(to), row_inside(come)

    for y in range(ROWS):
        xb[0, y, OWN:OWN + BLOCK, :] = x_ref[y]
    for y in ORDER:
        send(0, y)

    xb[:, :, EDGE + 3 * CH:DEPTH, :] = jnp.zeros((ROUNDS, ROWS, DEPTH - EDGE - 3 * CH, LANES), jnp.bfloat16)

    @pl.when(i < 2)
    def _():
        xb[:, :, 0:BLOCK, :] = jnp.zeros((ROUNDS, ROWS, BLOCK, LANES), jnp.bfloat16)
        xb[:, :, EDGE:EDGE + CH, :] = jnp.zeros((ROUNDS, ROWS, CH, LANES), jnp.bfloat16)

    @pl.when(i >= n_off - 2)
    def _():
        xb[:, :, 2 * BLOCK:3 * BLOCK, :] = jnp.zeros((ROUNDS, ROWS, BLOCK, LANES), jnp.bfloat16)
        xb[:, :, EDGE + 2 * CH:EDGE + 3 * CH, :] = jnp.zeros((ROUNDS, ROWS, CH, LANES), jnp.bfloat16)

    @pl.when(r == 0)
    def _():
        mixed[:, 0:BLOCK, :] = jnp.zeros((ROUNDS, BLOCK, LANES), jnp.bfloat16)

    @pl.when(r == n_rows - 1)
    def _():
        mixed[:, (ROWS + 1) * BLOCK:, :] = jnp.zeros((ROUNDS, BLOCK, LANES), jnp.bfloat16)

    row = lax.broadcasted_iota(jnp.int32, (BLOCK, BLOCK), 0)
    col = lax.broadcasted_iota(jnp.int32, (BLOCK, BLOCK), 1)
    v_out, v_in = row // CH, col // CH
    spread = (lax.broadcasted_iota(jnp.int32, (CH, BLOCK), 1) % CH
              == lax.broadcasted_iota(jnp.int32, (CH, BLOCK), 0)).astype(jnp.bfloat16)
    pick = (lax.broadcasted_iota(jnp.int32, (BLOCK, CH), 0) % CH
            == lax.broadcasted_iota(jnp.int32, (BLOCK, CH), 1))
    edge_row = (HALF - 1) * (1 - odd)
    for rnd in range(ROUNDS):
        for kind, (k_ref, b_ref) in enumerate(((ok_ref, ob_ref), (sk_ref, sb_ref))):
            bias[rnd, kind] = jnp.sum(jnp.where(pick, b_ref[rnd:rnd + 1, :], 0.0), axis=1, keepdims=True)
            wide = jnp.dot(k_ref[rnd], spread, preferred_element_type=jnp.float32)
            taps = [jnp.concatenate([wide[t * CH:(t + 1) * CH]] * HALF, axis=0) for t in range(9)]
            if kind == 0:
                edges = jnp.zeros((BLOCK, BLOCK), jnp.float32)
                for a in range(3):
                    block = jnp.zeros((BLOCK, BLOCK), jnp.float32)
                    for b in range(3):
                        block = jnp.where(v_in - v_out == b - 1, taps[3 * a + b], block)
                    w_off[rnd, :, a * BLOCK:(a + 1) * BLOCK] = block.astype(jnp.bfloat16)
                    outer = jnp.where(odd == 1, taps[3 * a], taps[3 * a + 2])
                    edges = jnp.where((v_in == a) & (v_out == edge_row), outer, edges)
                w_off[rnd, :, EDGE:DEPTH] = edges.astype(jnp.bfloat16)
            else:
                for a in range(3):
                    for b in range(3):
                        block = jnp.where(v_in == v_out, taps[3 * a + b], 0.0)
                        w_sp[rnd, b * BLOCK:(b + 1) * BLOCK, a * BLOCK:(a + 1) * BLOCK] = block.astype(jnp.bfloat16)

    image = lax.broadcasted_iota(jnp.int32, (BLOCK, LANES), 1) < WIDTH

    def mix(rnd, y):
        total = jnp.dot(w_off[rnd], xb[rnd, y], preferred_element_type=jnp.float32) + bias[rnd, 0]
        value = jnp.where(image, jnp.maximum(total, 0.0), 0.0)
        mixed[rnd, (y + 1) * BLOCK:(y + 2) * BLOCK, :] = value.astype(jnp.bfloat16)

    def spatial(rnd, y):
        parts = jnp.dot(w_sp[rnd], mixed[rnd, y * BLOCK:(y + 3) * BLOCK, :], preferred_element_type=jnp.float32)
        total = (pltpu.roll(parts[:BLOCK], 1, 1) + parts[BLOCK:2 * BLOCK]
                 + pltpu.roll(parts[2 * BLOCK:], LANES - 1, 1) + bias[rnd, 1])
        value = jnp.maximum(total, 0.0).astype(jnp.bfloat16)
        if rnd == 0:
            xb[1, y, OWN:OWN + BLOCK, :] = value
            send(1, y)
        else:
            o_ref[y] = value

    for rnd in range(ROUNDS):
        for y in ORDER:
            receive(rnd, y)
            mix(rnd, y)
            if y in (0, 3):
                copy, to, _ = halo(rnd, 0 if y == 0 else 1)

                @pl.when(to)
                def _():
                    copy.start()
            if y == 1:
                copy, _, come = halo(rnd, 1)

                @pl.when(come)
                def _():
                    copy.wait_recv()
                spatial(rnd, 0)
            if y == 2:
                copy, _, come = halo(rnd, 0)

                @pl.when(come)
                def _():
                    copy.wait_recv()
                for z in (3, 1, 2):
                    spatial(rnd, z)

    for rnd in range(ROUNDS):
        for y in range(ROWS):
            sent(rnd, y)
        for side in range(2):
            copy, to, _ = halo(rnd, side)

            @pl.when(to)
            def _():
                copy.wait_send()


def local(volume, offset_kernels, offset_biases, spatial_kernels, spatial_biases):
    n_off, n_rows = lax.axis_size("off"), lax.axis_size("rows")
    x = jnp.transpose(volume, (2, 0, 1, 3)).reshape(ROWS, BLOCK, WIDTH)
    x = jnp.pad(x, ((0, 0), (0, 0), (0, LANES - WIDTH)))
    vmem = pl.BlockSpec(memory_space=pltpu.VMEM)
    out = pl.pallas_call(
        lambda *refs: kernel(n_off, n_rows, *refs),
        out_shape=jax.ShapeDtypeStruct((ROWS, BLOCK, LANES), jnp.bfloat16),
        in_specs=[vmem] * 5,
        out_specs=vmem,
        scratch_shapes=[
            pltpu.VMEM((ROUNDS, ROWS, DEPTH, LANES), jnp.bfloat16),
            pltpu.VMEM((ROUNDS, (ROWS + 2) * BLOCK, LANES), jnp.bfloat16),
            pltpu.VMEM((ROUNDS, BLOCK, DEPTH), jnp.bfloat16),
            pltpu.VMEM((ROUNDS, 3 * BLOCK, 3 * BLOCK), jnp.bfloat16),
            pltpu.VMEM((ROUNDS, 2, BLOCK, 1), jnp.float32),
            pltpu.SemaphoreType.DMA((ROUNDS, ROWS, 5)),
            pltpu.SemaphoreType.DMA((ROUNDS, ROWS, 5)),
            pltpu.SemaphoreType.DMA((ROUNDS, 2)),
            pltpu.SemaphoreType.DMA((ROUNDS, 2)),
        ],
        compiler_params=pltpu.CompilerParams(collective_id=0, has_side_effects=True, vmem_limit_bytes=40 << 20),
        cost_estimate=pl.CostEstimate(flops=1 << 30, bytes_accessed=1 << 20, transcendentals=0),
        name="filter_rounds",
    )(x, offset_kernels.reshape(ROUNDS, 9 * CH, CH), offset_biases,
      spatial_kernels.reshape(ROUNDS, 9 * CH, CH), spatial_biases)
    out = out[:, :, :WIDTH].reshape(ROWS, HALF, CH, WIDTH)
    return jnp.transpose(out, (1, 2, 0, 3))


def solution(mesh):
    in_specs = (P("off", None, "rows", None), P(), P(), P(), P())
    out_specs = P("off", None, "rows", None)
    return jax.shard_map(local, mesh=mesh, in_specs=in_specs, out_specs=out_specs, check_vma=False)
```

```python
import jax
import jax.numpy as jnp
from jax import lax
from jax.experimental import pallas as pl
from jax.experimental.pallas import tpu as pltpu
from jax.sharding import PartitionSpec as P

MESH = pl.DeviceIdType.MESH
CH = 16
ROUNDS = 2
HALF = 8
BLOCK = HALF * CH
INNER = BLOCK - CH
ROWS = 4
WIDTH = 480
LANES = 512
WHOLE = 384
REST = 96
QUARTER = BLOCK - REST
OWN = BLOCK
ORDER = (0, 3, 1, 2)
FIRST = 3


def kernel(n_off, n_rows, x_hbm, ok_hbm, ob_hbm, sk_hbm, sb_hbm, o_ref,
           x_ref, ok_ref, ob_ref, sk_ref, sb_ref, ls,
           xb, mixed, packed, part_out, part_in, held, side_in, w_off, w_sp, bias,
           ss, rs, ps, pr, es, er, hs, hr):
    i, r = lax.axis_index("off"), lax.axis_index("rows")
    odd = lax.rem(i, 2)
    s = 1 - 2 * odd
    pair = i + s

    def inside(t):
        return (t >= 0) & (t < n_off)

    def row_inside(t):
        return (t >= 0) & (t < n_rows)

    loads = [pltpu.make_async_copy(a, b, ls.at[n]) for n, (a, b) in enumerate(
        ((x_hbm, x_ref), (ok_hbm, ok_ref), (ob_hbm, ob_ref), (sk_hbm, sk_ref), (sb_hbm, sb_ref)))]
    for load in loads:
        load.start()

    barrier = pltpu.get_barrier_semaphore()
    count = jnp.int32(1)
    pl.semaphore_signal(barrier, inc=1, device_id=(pair, r), device_id_type=MESH)
    for t in (i - 2, i + 2):
        @pl.when(inside(t))
        def _():
            pl.semaphore_signal(barrier, inc=1, device_id=(t, r), device_id_type=MESH)
        count = count + inside(t).astype(jnp.int32)
    for t in (r - 1, r + 1):
        @pl.when(row_inside(t))
        def _():
            pl.semaphore_signal(barrier, inc=1, device_id=(i, t), device_id_type=MESH)
        count = count + row_inside(t).astype(jnp.int32)

    def plane_at(p):
        return pl.multiple_of(CH * (p + odd * (HALF - 1 - 2 * p)), CH)

    lane = lax.broadcasted_iota(jnp.int32, (QUARTER, BLOCK), 1)

    def pack(rnd, y):
        n = QUARTER if rnd == 0 else CH
        last = xb[rnd, y, OWN + REST:OWN + REST + n, WHOLE:].astype(jnp.float32)
        for g in range(3):
            at = g * QUARTER
            keep = xb[rnd, y, OWN + at:OWN + at + n, WHOLE:]
            moved = pltpu.roll(last, REST - at, 1).astype(jnp.bfloat16)
            packed[rnd, y, at:at + n, :] = jnp.where(lane[:n] < REST, keep, moved)
            if n < QUARTER:
                packed[rnd, y, at + n:at + QUARTER, :] = xb[rnd, y, OWN + at + n:OWN + at + QUARTER, WHOLE:]

    def unpack(rnd, y, base):
        n = QUARTER if rnd == 0 else CH
        value = None
        for g in (2, 1, 0):
            at = base + g * QUARTER
            moved = pltpu.roll(xb[rnd, y, at:at + n, WHOLE:].astype(jnp.float32), (g + 1) * QUARTER, 1)
            value = moved if value is None else jnp.where(lane[:n] < (g + 1) * QUARTER, moved, value)
        xb[rnd, y, base + REST:base + REST + n, WHOLE:] = value.astype(jnp.bfloat16)

    sides = ((0, i + 2, i - 2), (2 * BLOCK, i - 2, i + 2))

    def flows(rnd, y):
        n = BLOCK if rnd == 0 else INNER
        for f, (at, to, come) in enumerate(sides):
            yield pltpu.make_async_remote_copy(
                src_ref=xb.at[rnd, y, pl.ds(OWN, n), pl.ds(0, WHOLE)],
                dst_ref=xb.at[rnd, y, pl.ds(at, n), pl.ds(0, WHOLE)],
                send_sem=ss.at[rnd, y, 2 * f], recv_sem=rs.at[rnd, y, 2 * f],
                device_id=(to, r), device_id_type=MESH), inside(to), inside(come)
            yield pltpu.make_async_remote_copy(
                src_ref=packed.at[rnd, y],
                dst_ref=xb.at[rnd, y, pl.ds(at, REST), pl.ds(WHOLE, BLOCK)],
                send_sem=ss.at[rnd, y, 2 * f + 1], recv_sem=rs.at[rnd, y, 2 * f + 1],
                device_id=(to, r), device_id_type=MESH), inside(to), inside(come)

    def edge_flows():
        for f, (at, to, come) in enumerate(sides):
            yield pltpu.make_async_remote_copy(
                src_ref=xb.at[1, :, pl.ds(OWN + INNER, CH)],
                dst_ref=xb.at[1, :, pl.ds(at + INNER, CH)],
                send_sem=es.at[f], recv_sem=er.at[f],
                device_id=(to, r), device_id_type=MESH), inside(to), inside(come)

    def start(copies):
        for copy, to, _ in copies:
            @pl.when(to)
            def _():
                copy.start()

    def sent(copies):
        for copy, to, _ in copies:
            @pl.when(to)
            def _():
                copy.wait_send()

    def arrived(copies):
        for copy, _, come in copies:
            @pl.when(come)
            def _():
                copy.wait_recv()

    def receive(rnd, y):
        arrived(flows(rnd, y))
        for at, _, come in sides:
            @pl.when(inside(come))
            def _():
                unpack(rnd, y, at)

    def partial_copy(rnd, y):
        return pltpu.make_async_remote_copy(
            src_ref=part_out.at[rnd, y], dst_ref=part_in.at[rnd, y],
            send_sem=ps.at[rnd, y], recv_sem=pr.at[rnd, y],
            device_id=(pair, r), device_id_type=MESH)

    def halo(rnd, side, kind):
        src, dst, to, come = ((1, ROWS + 1, r - 1, r + 1), (ROWS, 0, r + 1, r - 1))[side]
        if kind == 0:
            ends = (mixed.at[rnd, pl.ds(src * BLOCK, INNER), :], mixed.at[rnd, pl.ds(dst * BLOCK, INNER), :])
        else:
            ends = (mixed.at[rnd, pl.ds(src * BLOCK + INNER, CH), :], side_in.at[rnd, side])
        return [(pltpu.make_async_remote_copy(
            src_ref=ends[0], dst_ref=ends[1], send_sem=hs.at[rnd, side, kind], recv_sem=hr.at[rnd, side, kind],
            device_id=(i, to), device_id_type=MESH), row_inside(to), row_inside(come))]

    loads[0].wait()
    for y in ORDER:
        for p in range(HALF):
            xb[0, y, OWN + p * CH:OWN + (p + 1) * CH, 0:WIDTH] = x_ref[pl.ds(plane_at(p), CH), y, :]
        pack(0, y)
        if y == ORDER[0]:
            pl.semaphore_wait(barrier, count)
        if y in ORDER[:FIRST]:
            start(flows(0, y))

    for rnd in range(ROUNDS):
        for y in range(ROWS):
            @pl.when(i < 2)
            def _():
                xb[rnd, y, 0:BLOCK, :] = jnp.zeros((BLOCK, LANES), jnp.bfloat16)

            @pl.when(i >= n_off - 2)
            def _():
                xb[rnd, y, 2 * BLOCK:, :] = jnp.zeros((BLOCK, LANES), jnp.bfloat16)

        mixed[rnd, INNER:BLOCK, :] = jnp.zeros((CH, LANES), jnp.bfloat16)
        mixed[rnd, (ROWS + 1) * BLOCK + INNER:, :] = jnp.zeros((CH, LANES), jnp.bfloat16)

        @pl.when(r == 0)
        def _():
            mixed[rnd, 0:INNER, :] = jnp.zeros((INNER, LANES), jnp.bfloat16)

        @pl.when(r == n_rows - 1)
        def _():
            mixed[rnd, (ROWS + 1) * BLOCK:(ROWS + 1) * BLOCK + INNER, :] = jnp.zeros((INNER, LANES), jnp.bfloat16)

    row = lax.broadcasted_iota(jnp.int32, (BLOCK, BLOCK), 0)
    col = lax.broadcasted_iota(jnp.int32, (BLOCK, BLOCK), 1)
    p_out, p_in = row // CH, col // CH
    spread = (lax.broadcasted_iota(jnp.int32, (CH, BLOCK), 1) % CH
              == lax.broadcasted_iota(jnp.int32, (CH, BLOCK), 0)).astype(jnp.bfloat16)
    pick = (lax.broadcasted_iota(jnp.int32, (BLOCK, CH), 0) % CH
            == lax.broadcasted_iota(jnp.int32, (BLOCK, CH), 1))
    for load in loads[1:]:
        load.wait()
    for rnd in range(ROUNDS):
        for kind, (k_ref, b_ref) in enumerate(((ok_ref, ob_ref), (sk_ref, sb_ref))):
            bias[rnd, kind] = jnp.sum(jnp.where(pick, b_ref[rnd:rnd + 1, :], 0.0), axis=1, keepdims=True)
            wide = jnp.dot(k_ref[rnd], spread, preferred_element_type=jnp.float32)
            taps = [wide[t * CH:(t + 1) * CH] for t in range(9)]
            full = [jnp.concatenate([tap] * HALF, axis=0) for tap in taps]
            for a in range(3):
                if kind == 0:
                    block = jnp.zeros((BLOCK, BLOCK), jnp.float32)
                    for b in range(3):
                        block = jnp.where(p_in - p_out == s * (b - 1), full[3 * a + b], block)
                    w_off[rnd, 0:BLOCK, a * BLOCK:(a + 1) * BLOCK] = block.astype(jnp.bfloat16)
                    outer = jnp.where(odd == 1, taps[3 * a + 2], taps[3 * a])
                    outer = jnp.where(p_in[:CH] == HALF - 1, outer, 0.0)
                    w_off[rnd, BLOCK:, a * BLOCK:(a + 1) * BLOCK] = outer.astype(jnp.bfloat16)
                else:
                    for b in range(3):
                        block = jnp.where(p_in == p_out, full[3 * a + b], 0.0)
                        w_sp[rnd, b * BLOCK:(b + 1) * BLOCK, a * BLOCK:(a + 1) * BLOCK] = block.astype(jnp.bfloat16)

    image = lax.broadcasted_iota(jnp.int32, (BLOCK, LANES), 1) < WIDTH

    def mix(rnd, y):
        sums = jnp.dot(w_off[rnd], xb[rnd, y], preferred_element_type=jnp.float32)
        part_out[rnd, y] = sums[BLOCK:].astype(jnp.bfloat16)
        partial_copy(rnd, y).start()
        sums = sums[:BLOCK] + bias[rnd, 0]
        held[y] = sums[INNER:]
        value = jnp.where(image, jnp.maximum(sums, 0.0), 0.0)
        mixed[rnd, (y + 1) * BLOCK:(y + 2) * BLOCK, :] = value.astype(jnp.bfloat16)
        if y in (0, ROWS - 1):
            start(halo(rnd, 0 if y == 0 else 1, 0))

    def mix_last(rnd, y):
        partial_copy(rnd, y).wait_recv()
        sums = held[y] + part_in[rnd, y].astype(jnp.float32)
        value = jnp.where(image[:CH], jnp.maximum(sums, 0.0), 0.0)
        mixed[rnd, (y + 1) * BLOCK + INNER:(y + 2) * BLOCK, :] = value.astype(jnp.bfloat16)
        if y in (0, ROWS - 1):
            start(halo(rnd, 0 if y == 0 else 1, 1))

    def filtered(parts, biases):
        n = parts.shape[0] // 3
        sums = (pltpu.roll(parts[:n], 1, 1) + parts[n:2 * n]
                + pltpu.roll(parts[2 * n:], LANES - 1, 1) + biases)
        return jnp.maximum(sums, 0.0).astype(jnp.bfloat16)

    def spatial(rnd, y):
        parts = jnp.dot(w_sp[rnd], mixed[rnd, y * BLOCK:(y + 3) * BLOCK, :], preferred_element_type=jnp.float32)
        value = filtered(parts, bias[rnd, 1])
        if rnd == 0:
            xb[1, y, OWN:OWN + INNER, :] = value[:INNER]
            pack(1, y)
        else:
            for p in range(HALF - 1):
                o_ref[y, pl.ds(plane_at(p), CH), :] = value[p * CH:(p + 1) * CH]

    def spatial_last(rnd):
        for side in range(2):
            dst = (ROWS + 1, 0)[side]

            @pl.when(row_inside((r + 1, r - 1)[side]))
            def _():
                mixed[rnd, dst * BLOCK + INNER:(dst + 1) * BLOCK, :] = side_in[rnd, side]
        weights = jnp.concatenate([w_sp[rnd, b * BLOCK + INNER:(b + 1) * BLOCK, :] for b in range(3)], axis=0)
        for y in range(ROWS):
            parts = jnp.dot(weights, mixed[rnd, y * BLOCK:(y + 3) * BLOCK, :], preferred_element_type=jnp.float32)
            value = filtered(parts, bias[rnd, 1, INNER:])
            if rnd == 0:
                xb[1, y, OWN + INNER:OWN + BLOCK, :] = value
            else:
                o_ref[y, pl.ds(plane_at(HALF - 1), CH), :] = value

    for rnd in range(ROUNDS):
        for n, y in enumerate(ORDER):
            receive(rnd, y)
            if rnd == 1 and n == 0:
                arrived(edge_flows())
            mix(rnd, y)
            if rnd == 0 and n + FIRST < ROWS:
                start(flows(0, ORDER[n + FIRST]))
            if n == 2:
                arrived(halo(rnd, 1, 0))
                spatial(rnd, 0)
                if rnd == 0:
                    start(flows(1, 0))
            if n == 3:
                arrived(halo(rnd, 0, 0))
                spatial(rnd, 3)
                if rnd == 0:
                    start(flows(1, 3))
                spatial(rnd, 1)
                spatial(rnd, 2)
            if n > 0:
                mix_last(rnd, ORDER[n - 1])
        mix_last(rnd, ORDER[-1])
        for side in range(2):
            arrived(halo(rnd, side, 1))
        spatial_last(rnd)
        if rnd == 0:
            start(edge_flows())
            start(flows(1, 1))
            start(flows(1, 2))

    sent(edge_flows())
    for rnd in range(ROUNDS):
        for y in range(ROWS):
            sent(flows(rnd, y))
            partial_copy(rnd, y).wait_send()
        for side in range(2):
            for kind in range(2):
                sent(halo(rnd, side, kind))


def local(volume, offset_kernels, offset_biases, spatial_kernels, spatial_biases):
    n_off, n_rows = lax.axis_size("off"), lax.axis_size("rows")
    out = pl.pallas_call(
        lambda *refs: kernel(n_off, n_rows, *refs),
        out_shape=jax.ShapeDtypeStruct((ROWS, BLOCK, LANES), jnp.bfloat16),
        in_specs=[pl.BlockSpec(memory_space=pltpu.HBM)] * 5,
        out_specs=pl.BlockSpec(memory_space=pltpu.VMEM),
        scratch_shapes=[
            pltpu.VMEM((BLOCK, ROWS, WIDTH), jnp.bfloat16),
            pltpu.VMEM((ROUNDS, 9 * CH, CH), jnp.bfloat16),
            pltpu.VMEM((ROUNDS, CH), jnp.float32),
            pltpu.VMEM((ROUNDS, 9 * CH, CH), jnp.bfloat16),
            pltpu.VMEM((ROUNDS, CH), jnp.float32),
            pltpu.SemaphoreType.DMA((5,)),
            pltpu.VMEM((ROUNDS, ROWS, 3 * BLOCK, LANES), jnp.bfloat16),
            pltpu.VMEM((ROUNDS, (ROWS + 2) * BLOCK, LANES), jnp.bfloat16),
            pltpu.VMEM((ROUNDS, ROWS, REST, BLOCK), jnp.bfloat16),
            pltpu.VMEM((ROUNDS, ROWS, CH, LANES), jnp.bfloat16),
            pltpu.VMEM((ROUNDS, ROWS, CH, LANES), jnp.bfloat16),
            pltpu.VMEM((ROWS, CH, LANES), jnp.float32),
            pltpu.VMEM((ROUNDS, 2, CH, LANES), jnp.bfloat16),
            pltpu.VMEM((ROUNDS, BLOCK + CH, 3 * BLOCK), jnp.bfloat16),
            pltpu.VMEM((ROUNDS, 3 * BLOCK, 3 * BLOCK), jnp.bfloat16),
            pltpu.VMEM((ROUNDS, 2, BLOCK, 1), jnp.float32),
            pltpu.SemaphoreType.DMA((ROUNDS, ROWS, 4)),
            pltpu.SemaphoreType.DMA((ROUNDS, ROWS, 4)),
            pltpu.SemaphoreType.DMA((ROUNDS, ROWS)),
            pltpu.SemaphoreType.DMA((ROUNDS, ROWS)),
            pltpu.SemaphoreType.DMA((2,)),
            pltpu.SemaphoreType.DMA((2,)),
            pltpu.SemaphoreType.DMA((ROUNDS, 2, 2)),
            pltpu.SemaphoreType.DMA((ROUNDS, 2, 2)),
        ],
        compiler_params=pltpu.CompilerParams(collective_id=0, has_side_effects=True, vmem_limit_bytes=64 << 20),
        cost_estimate=pl.CostEstimate(flops=1 << 30, bytes_accessed=1 << 20, transcendentals=0),
        name="filter_rounds",
    )(volume.reshape(BLOCK, ROWS, WIDTH), offset_kernels.reshape(ROUNDS, 9 * CH, CH), offset_biases,
      spatial_kernels.reshape(ROUNDS, 9 * CH, CH), spatial_biases)
    out = out[:, :, :WIDTH].reshape(ROWS, HALF, CH, WIDTH)
    return jnp.transpose(out, (1, 2, 0, 3))


def solution(mesh):
    in_specs = (P("off", None, "rows", None), P(), P(), P(), P())
    out_specs = P("off", None, "rows", None)
    return jax.shard_map(local, mesh=mesh, in_specs=in_specs, out_specs=out_specs, check_vma=False)
```

```python
import jax
import jax.numpy as jnp
from jax import lax
from jax.experimental import pallas as pl
from jax.experimental.pallas import tpu as pltpu
from jax.sharding import PartitionSpec as P

MESH = pl.DeviceIdType.MESH
CH = 16
ROUNDS = 2
HALF = 8
BLOCK = HALF * CH
INNER = BLOCK - CH
ROWS = 4
WIDTH = 480
LANES = 512
WHOLE = 384
REST = 96
QUARTER = BLOCK - REST
OWN = BLOCK
ORDER = (0, 3, 1, 2)
FIRST = 3


def kernel(n_off, n_rows, x_hbm, ok_hbm, ob_hbm, sk_hbm, sb_hbm, o_ref,
           x_ref, ok_ref, ob_ref, sk_ref, sb_ref, ls,
           xb, mixed, packed, part_out, part_in, held, side_in, w_off, w_sp, bias,
           ss, rs, ps, pr, es, er, hs, hr):
    i, r = lax.axis_index("off"), lax.axis_index("rows")
    odd = lax.rem(i, 2)
    s = 1 - 2 * odd
    pair = i + s

    def inside(t):
        return (t >= 0) & (t < n_off)

    def row_inside(t):
        return (t >= 0) & (t < n_rows)

    loads = [pltpu.make_async_copy(a, b, ls.at[n]) for n, (a, b) in enumerate(
        ((x_hbm, x_ref), (ok_hbm, ok_ref), (ob_hbm, ob_ref), (sk_hbm, sk_ref), (sb_hbm, sb_ref)))]
    for load in loads:
        load.start()

    barrier = pltpu.get_barrier_semaphore()
    count = jnp.int32(1)
    pl.semaphore_signal(barrier, inc=1, device_id=(pair, r), device_id_type=MESH)
    for t in (i - 2, i + 2):
        @pl.when(inside(t))
        def _():
            pl.semaphore_signal(barrier, inc=1, device_id=(t, r), device_id_type=MESH)
        count = count + inside(t).astype(jnp.int32)
    for t in (r - 1, r + 1):
        @pl.when(row_inside(t))
        def _():
            pl.semaphore_signal(barrier, inc=1, device_id=(i, t), device_id_type=MESH)
        count = count + row_inside(t).astype(jnp.int32)

    def plane_at(p):
        return pl.multiple_of(CH * (p + odd * (HALF - 1 - 2 * p)), CH)

    lane = lax.broadcasted_iota(jnp.int32, (QUARTER, BLOCK), 1)

    def pack(rnd, y):
        n = QUARTER if rnd == 0 else CH
        last = xb[rnd, y, OWN + REST:OWN + REST + n, WHOLE:].astype(jnp.float32)
        for g in range(3):
            at = g * QUARTER
            keep = xb[rnd, y, OWN + at:OWN + at + n, WHOLE:]
            moved = pltpu.roll(last, REST - at, 1).astype(jnp.bfloat16)
            packed[rnd, y, at:at + n, :] = jnp.where(lane[:n] < REST, keep, moved)
            if n < QUARTER:
                packed[rnd, y, at + n:at + QUARTER, :] = xb[rnd, y, OWN + at + n:OWN + at + QUARTER, WHOLE:]

    def unpack(rnd, y, base):
        n = QUARTER if rnd == 0 else CH
        value = None
        for g in (2, 1, 0):
            at = base + g * QUARTER
            moved = pltpu.roll(xb[rnd, y, at:at + n, WHOLE:].astype(jnp.float32), (g + 1) * QUARTER, 1)
            value = moved if value is None else jnp.where(lane[:n] < (g + 1) * QUARTER, moved, value)
        xb[rnd, y, base + REST:base + REST + n, WHOLE:] = value.astype(jnp.bfloat16)

    sides = ((0, i + 2, i - 2), (2 * BLOCK, i - 2, i + 2))

    def flows(rnd, y):
        n = BLOCK if rnd == 0 else INNER
        for f, (at, to, come) in enumerate(sides):
            yield pltpu.make_async_remote_copy(
                src_ref=xb.at[rnd, y, pl.ds(OWN, n), pl.ds(0, WHOLE)],
                dst_ref=xb.at[rnd, y, pl.ds(at, n), pl.ds(0, WHOLE)],
                send_sem=ss.at[rnd, y, 2 * f], recv_sem=rs.at[rnd, y, 2 * f],
                device_id=(to, r), device_id_type=MESH), inside(to), inside(come)
            yield pltpu.make_async_remote_copy(
                src_ref=packed.at[rnd, y],
                dst_ref=xb.at[rnd, y, pl.ds(at, REST), pl.ds(WHOLE, BLOCK)],
                send_sem=ss.at[rnd, y, 2 * f + 1], recv_sem=rs.at[rnd, y, 2 * f + 1],
                device_id=(to, r), device_id_type=MESH), inside(to), inside(come)

    def edge_flows():
        for f, (at, to, come) in enumerate(sides):
            yield pltpu.make_async_remote_copy(
                src_ref=xb.at[1, :, pl.ds(OWN + INNER, CH)],
                dst_ref=xb.at[1, :, pl.ds(at + INNER, CH)],
                send_sem=es.at[f], recv_sem=er.at[f],
                device_id=(to, r), device_id_type=MESH), inside(to), inside(come)

    def start(copies):
        for copy, to, _ in copies:
            @pl.when(to)
            def _():
                copy.start()

    def sent(copies):
        for copy, to, _ in copies:
            @pl.when(to)
            def _():
                copy.wait_send()

    def arrived(copies):
        for copy, _, come in copies:
            @pl.when(come)
            def _():
                copy.wait_recv()

    def receive(rnd, y):
        arrived(flows(rnd, y))
        for at, _, come in sides:
            @pl.when(inside(come))
            def _():
                unpack(rnd, y, at)

    def partial_copy(rnd, y):
        return pltpu.make_async_remote_copy(
            src_ref=part_out.at[rnd, y], dst_ref=part_in.at[rnd, y],
            send_sem=ps.at[rnd, y], recv_sem=pr.at[rnd, y],
            device_id=(pair, r), device_id_type=MESH)

    def halo(rnd, side, kind):
        src, dst, to, come = ((1, ROWS + 1, r - 1, r + 1), (ROWS, 0, r + 1, r - 1))[side]
        if kind == 0:
            ends = (mixed.at[rnd, pl.ds(src * BLOCK, INNER), :], mixed.at[rnd, pl.ds(dst * BLOCK, INNER), :])
        else:
            ends = (mixed.at[rnd, pl.ds(src * BLOCK + INNER, CH), :], side_in.at[rnd, side])
        return [(pltpu.make_async_remote_copy(
            src_ref=ends[0], dst_ref=ends[1], send_sem=hs.at[rnd, side, kind], recv_sem=hr.at[rnd, side, kind],
            device_id=(i, to), device_id_type=MESH), row_inside(to), row_inside(come))]

    loads[0].wait()
    for y in ORDER:
        for p in range(HALF):
            xb[0, y, OWN + p * CH:OWN + (p + 1) * CH, 0:WIDTH] = x_ref[pl.ds(plane_at(p), CH), y, :]
        pack(0, y)
        if y == ORDER[0]:
            pl.semaphore_wait(barrier, count)
        if y in ORDER[:FIRST]:
            start(flows(0, y))

    for rnd in range(ROUNDS):
        for y in range(ROWS):
            @pl.when(i < 2)
            def _():
                xb[rnd, y, 0:BLOCK, :] = jnp.zeros((BLOCK, LANES), jnp.bfloat16)

            @pl.when(i >= n_off - 2)
            def _():
                xb[rnd, y, 2 * BLOCK:, :] = jnp.zeros((BLOCK, LANES), jnp.bfloat16)

        mixed[rnd, INNER:BLOCK, :] = jnp.zeros((CH, LANES), jnp.bfloat16)
        mixed[rnd, (ROWS + 1) * BLOCK + INNER:, :] = jnp.zeros((CH, LANES), jnp.bfloat16)

        @pl.when(r == 0)
        def _():
            mixed[rnd, 0:INNER, :] = jnp.zeros((INNER, LANES), jnp.bfloat16)

        @pl.when(r == n_rows - 1)
        def _():
            mixed[rnd, (ROWS + 1) * BLOCK:(ROWS + 1) * BLOCK + INNER, :] = jnp.zeros((INNER, LANES), jnp.bfloat16)

    row = lax.broadcasted_iota(jnp.int32, (BLOCK, BLOCK), 0)
    col = lax.broadcasted_iota(jnp.int32, (BLOCK, BLOCK), 1)
    p_out, p_in = row // CH, col // CH
    spread = (lax.broadcasted_iota(jnp.int32, (CH, BLOCK), 1) % CH
              == lax.broadcasted_iota(jnp.int32, (CH, BLOCK), 0)).astype(jnp.bfloat16)
    pick = (lax.broadcasted_iota(jnp.int32, (BLOCK, CH), 0) % CH
            == lax.broadcasted_iota(jnp.int32, (BLOCK, CH), 1))
    for load in loads[1:]:
        load.wait()
    for rnd in range(ROUNDS):
        for kind, (k_ref, b_ref) in enumerate(((ok_ref, ob_ref), (sk_ref, sb_ref))):
            bias[rnd, kind] = jnp.sum(jnp.where(pick, b_ref[rnd:rnd + 1, :], 0.0), axis=1, keepdims=True)
            wide = jnp.dot(k_ref[rnd], spread, preferred_element_type=jnp.float32)
            taps = [wide[t * CH:(t + 1) * CH] for t in range(9)]
            full = [jnp.concatenate([tap] * HALF, axis=0) for tap in taps]
            for a in range(3):
                if kind == 0:
                    block = jnp.zeros((BLOCK, BLOCK), jnp.float32)
                    for b in range(3):
                        block = jnp.where(p_in - p_out == s * (b - 1), full[3 * a + b], block)
                    w_off[rnd, 0:BLOCK, a * BLOCK:(a + 1) * BLOCK] = block.astype(jnp.bfloat16)
                    outer = jnp.where(odd == 1, taps[3 * a + 2], taps[3 * a])
                    outer = jnp.where(p_in[:CH] == HALF - 1, outer, 0.0)
                    w_off[rnd, BLOCK:, a * BLOCK:(a + 1) * BLOCK] = outer.astype(jnp.bfloat16)
                else:
                    for b in range(3):
                        block = jnp.where(p_in == p_out, full[3 * a + b], 0.0)
                        w_sp[rnd, b * BLOCK:(b + 1) * BLOCK, a * BLOCK:(a + 1) * BLOCK] = block.astype(jnp.bfloat16)

    image = lax.broadcasted_iota(jnp.int32, (BLOCK, LANES), 1) < WIDTH

    def mix(rnd, y):
        sums = jnp.dot(w_off[rnd], xb[rnd, y], preferred_element_type=jnp.float32)
        part_out[rnd, y] = sums[BLOCK:].astype(jnp.bfloat16)
        partial_copy(rnd, y).start()
        sums = sums[:BLOCK] + bias[rnd, 0]
        held[y] = sums[INNER:]
        value = jnp.where(image, jnp.maximum(sums, 0.0), 0.0)
        mixed[rnd, (y + 1) * BLOCK:(y + 2) * BLOCK, :] = value.astype(jnp.bfloat16)
        if y in (0, ROWS - 1):
            start(halo(rnd, 0 if y == 0 else 1, 0))

    def mix_last(rnd, y):
        partial_copy(rnd, y).wait_recv()
        sums = held[y] + part_in[rnd, y].astype(jnp.float32)
        value = jnp.where(image[:CH], jnp.maximum(sums, 0.0), 0.0)
        mixed[rnd, (y + 1) * BLOCK + INNER:(y + 2) * BLOCK, :] = value.astype(jnp.bfloat16)
        if y in (0, ROWS - 1):
            start(halo(rnd, 0 if y == 0 else 1, 1))

    def filtered(parts, biases):
        n = parts.shape[0] // 3
        sums = (pltpu.roll(parts[:n], 1, 1) + parts[n:2 * n]
                + pltpu.roll(parts[2 * n:], LANES - 1, 1) + biases)
        return jnp.maximum(sums, 0.0).astype(jnp.bfloat16)

    def spatial(rnd, y):
        parts = jnp.dot(w_sp[rnd], mixed[rnd, y * BLOCK:(y + 3) * BLOCK, :], preferred_element_type=jnp.float32)
        value = filtered(parts, bias[rnd, 1])
        if rnd == 0:
            xb[1, y, OWN:OWN + INNER, :] = value[:INNER]
            pack(1, y)
        else:
            for p in range(HALF - 1):
                o_ref[pl.ds(plane_at(p), CH), y, :] = value[p * CH:(p + 1) * CH, :WIDTH]

    def spatial_last(rnd):
        for side in range(2):
            dst = (ROWS + 1, 0)[side]

            @pl.when(row_inside((r + 1, r - 1)[side]))
            def _():
                mixed[rnd, dst * BLOCK + INNER:(dst + 1) * BLOCK, :] = side_in[rnd, side]
        weights = jnp.concatenate([w_sp[rnd, b * BLOCK + INNER:(b + 1) * BLOCK, :] for b in range(3)], axis=0)
        for y in range(ROWS):
            parts = jnp.dot(weights, mixed[rnd, y * BLOCK:(y + 3) * BLOCK, :], preferred_element_type=jnp.float32)
            value = filtered(parts, bias[rnd, 1, INNER:])
            if rnd == 0:
                xb[1, y, OWN + INNER:OWN + BLOCK, :] = value
            else:
                o_ref[pl.ds(plane_at(HALF - 1), CH), y, :] = value[:, :WIDTH]

    for rnd in range(ROUNDS):
        for n, y in enumerate(ORDER):
            receive(rnd, y)
            if rnd == 1 and n == 0:
                arrived(edge_flows())
            mix(rnd, y)
            if rnd == 0 and n + FIRST < ROWS:
                start(flows(0, ORDER[n + FIRST]))
            if n == 2:
                arrived(halo(rnd, 1, 0))
                spatial(rnd, 0)
                if rnd == 0:
                    start(flows(1, 0))
            if n == 3:
                arrived(halo(rnd, 0, 0))
                spatial(rnd, 3)
                if rnd == 0:
                    start(flows(1, 3))
                spatial(rnd, 1)
                spatial(rnd, 2)
            if n > 0:
                mix_last(rnd, ORDER[n - 1])
        mix_last(rnd, ORDER[-1])
        for side in range(2):
            arrived(halo(rnd, side, 1))
        spatial_last(rnd)
        if rnd == 0:
            start(edge_flows())
            start(flows(1, 1))
            start(flows(1, 2))

    sent(edge_flows())
    for rnd in range(ROUNDS):
        for y in range(ROWS):
            sent(flows(rnd, y))
            partial_copy(rnd, y).wait_send()
        for side in range(2):
            for kind in range(2):
                sent(halo(rnd, side, kind))


def local(volume, offset_kernels, offset_biases, spatial_kernels, spatial_biases):
    n_off, n_rows = lax.axis_size("off"), lax.axis_size("rows")
    out = pl.pallas_call(
        lambda *refs: kernel(n_off, n_rows, *refs),
        out_shape=pltpu.VMEM((BLOCK, ROWS, WIDTH), jnp.bfloat16),
        in_specs=[pl.BlockSpec(memory_space=pltpu.HBM)] * 5,
        out_specs=pl.BlockSpec(memory_space=pltpu.VMEM),
        scratch_shapes=[
            pltpu.VMEM((BLOCK, ROWS, WIDTH), jnp.bfloat16),
            pltpu.VMEM((ROUNDS, 9 * CH, CH), jnp.bfloat16),
            pltpu.VMEM((ROUNDS, CH), jnp.float32),
            pltpu.VMEM((ROUNDS, 9 * CH, CH), jnp.bfloat16),
            pltpu.VMEM((ROUNDS, CH), jnp.float32),
            pltpu.SemaphoreType.DMA((5,)),
            pltpu.VMEM((ROUNDS, ROWS, 3 * BLOCK, LANES), jnp.bfloat16),
            pltpu.VMEM((ROUNDS, (ROWS + 2) * BLOCK, LANES), jnp.bfloat16),
            pltpu.VMEM((ROUNDS, ROWS, REST, BLOCK), jnp.bfloat16),
            pltpu.VMEM((ROUNDS, ROWS, CH, LANES), jnp.bfloat16),
            pltpu.VMEM((ROUNDS, ROWS, CH, LANES), jnp.bfloat16),
            pltpu.VMEM((ROWS, CH, LANES), jnp.float32),
            pltpu.VMEM((ROUNDS, 2, CH, LANES), jnp.bfloat16),
            pltpu.VMEM((ROUNDS, BLOCK + CH, 3 * BLOCK), jnp.bfloat16),
            pltpu.VMEM((ROUNDS, 3 * BLOCK, 3 * BLOCK), jnp.bfloat16),
            pltpu.VMEM((ROUNDS, 2, BLOCK, 1), jnp.float32),
            pltpu.SemaphoreType.DMA((ROUNDS, ROWS, 4)),
            pltpu.SemaphoreType.DMA((ROUNDS, ROWS, 4)),
            pltpu.SemaphoreType.DMA((ROUNDS, ROWS)),
            pltpu.SemaphoreType.DMA((ROUNDS, ROWS)),
            pltpu.SemaphoreType.DMA((2,)),
            pltpu.SemaphoreType.DMA((2,)),
            pltpu.SemaphoreType.DMA((ROUNDS, 2, 2)),
            pltpu.SemaphoreType.DMA((ROUNDS, 2, 2)),
        ],
        compiler_params=pltpu.CompilerParams(collective_id=0, has_side_effects=True, vmem_limit_bytes=40 << 20),
        cost_estimate=pl.CostEstimate(flops=1 << 30, bytes_accessed=1 << 20, transcendentals=0),
        name="filter_rounds",
    )(*[pltpu.with_memory_space_constraint(a, pltpu.HBM) for a in (
        volume.reshape(BLOCK, ROWS, WIDTH), offset_kernels.reshape(ROUNDS, 9 * CH, CH), offset_biases,
        spatial_kernels.reshape(ROUNDS, 9 * CH, CH), spatial_biases)])
    return out.reshape(HALF, CH, ROWS, WIDTH)


def solution(mesh):
    in_specs = (P("off", None, "rows", None), P(), P(), P(), P())
    out_specs = P("off", None, "rows", None)
    return jax.shard_map(local, mesh=mesh, in_specs=in_specs, out_specs=out_specs, check_vma=False)
```

```python
import jax
import jax.numpy as jnp
from jax import lax
from jax.experimental import pallas as pl
from jax.experimental.pallas import tpu as pltpu
from jax.sharding import PartitionSpec as P

MESH = pl.DeviceIdType.MESH
CH = 16
ROUNDS = 2
HALF = 8
BLOCK = HALF * CH
INNER = BLOCK - CH
ROWS = 4
WIDTH = 480
LANES = 512
WHOLE = 384
REST = 96
QUARTER = BLOCK - REST
OWN = BLOCK
ORDER = (0, 3, 1, 2)
LAST = ORDER[-1]
FIRST = 3


def kernel(n_off, n_rows, x_hbm, ok_hbm, ob_hbm, sk_hbm, sb_hbm, o_ref,
           x_ref, ok_ref, ob_ref, sk_ref, sb_ref, ls,
           xb, mixed, packed, part_out, part_in, held, side_in, raw_in, w_off, w_sp, w_raw, bias,
           ss, rs, ps, pr, es, er, hs, hr, ws, wr):
    i, r = lax.axis_index("off"), lax.axis_index("rows")
    odd = lax.rem(i, 2)
    s = 1 - 2 * odd
    pair = i + s

    def inside(t):
        return (t >= 0) & (t < n_off)

    def row_inside(t):
        return (t >= 0) & (t < n_rows)

    loads = [pltpu.make_async_copy(a, b, ls.at[n]) for n, (a, b) in enumerate(
        ((x_hbm, x_ref), (ok_hbm, ok_ref), (ob_hbm, ob_ref), (sk_hbm, sk_ref), (sb_hbm, sb_ref)))]
    for load in loads:
        load.start()

    barrier = pltpu.get_barrier_semaphore()
    count = jnp.int32(1)
    pl.semaphore_signal(barrier, inc=1, device_id=(pair, r), device_id_type=MESH)
    for t in (i - 2, i + 2, i - s, i + 3 * s):
        @pl.when(inside(t))
        def _():
            pl.semaphore_signal(barrier, inc=1, device_id=(t, r), device_id_type=MESH)
        count = count + inside(t).astype(jnp.int32)
    for t in (r - 1, r + 1):
        @pl.when(row_inside(t))
        def _():
            pl.semaphore_signal(barrier, inc=1, device_id=(i, t), device_id_type=MESH)
        count = count + row_inside(t).astype(jnp.int32)

    def plane_at(p):
        return pl.multiple_of(CH * (p + odd * (HALF - 1 - 2 * p)), CH)

    lane = lax.broadcasted_iota(jnp.int32, (QUARTER, BLOCK), 1)

    def pack(rnd, y):
        n = QUARTER if rnd == 0 else CH
        last = xb[rnd, y, OWN + REST:OWN + REST + n, WHOLE:].astype(jnp.float32)
        for g in range(3):
            at = g * QUARTER
            keep = xb[rnd, y, OWN + at:OWN + at + n, WHOLE:]
            moved = pltpu.roll(last, REST - at, 1).astype(jnp.bfloat16)
            packed[rnd, y, at:at + n, :] = jnp.where(lane[:n] < REST, keep, moved)
            if n < QUARTER:
                packed[rnd, y, at + n:at + QUARTER, :] = xb[rnd, y, OWN + at + n:OWN + at + QUARTER, WHOLE:]

    def unpack(rnd, y, base):
        n = QUARTER if rnd == 0 else CH
        value = None
        for g in (2, 1, 0):
            at = base + g * QUARTER
            moved = pltpu.roll(xb[rnd, y, at:at + n, WHOLE:].astype(jnp.float32), (g + 1) * QUARTER, 1)
            value = moved if value is None else jnp.where(lane[:n] < (g + 1) * QUARTER, moved, value)
        xb[rnd, y, base + REST:base + REST + n, WHOLE:] = value.astype(jnp.bfloat16)

    sides = ((0, i + 2, i - 2), (2 * BLOCK, i - 2, i + 2))

    def flows(rnd, y):
        n = BLOCK if rnd == 0 else INNER
        for f, (at, to, come) in enumerate(sides):
            yield pltpu.make_async_remote_copy(
                src_ref=xb.at[rnd, y, pl.ds(OWN, n), pl.ds(0, WHOLE)],
                dst_ref=xb.at[rnd, y, pl.ds(at, n), pl.ds(0, WHOLE)],
                send_sem=ss.at[rnd, y, 2 * f], recv_sem=rs.at[rnd, y, 2 * f],
                device_id=(to, r), device_id_type=MESH), inside(to), inside(come)
            yield pltpu.make_async_remote_copy(
                src_ref=packed.at[rnd, y],
                dst_ref=xb.at[rnd, y, pl.ds(at, REST), pl.ds(WHOLE, BLOCK)],
                send_sem=ss.at[rnd, y, 2 * f + 1], recv_sem=rs.at[rnd, y, 2 * f + 1],
                device_id=(to, r), device_id_type=MESH), inside(to), inside(come)

    def edge_flows():
        for f, (at, to, come) in enumerate(sides):
            yield pltpu.make_async_remote_copy(
                src_ref=xb.at[1, :, pl.ds(OWN + INNER, CH)],
                dst_ref=xb.at[1, :, pl.ds(at + INNER, CH)],
                send_sem=es.at[f], recv_sem=er.at[f],
                device_id=(to, r), device_id_type=MESH), inside(to), inside(come)

    def raw_flows():
        for f, (slot, to) in enumerate(((1, pair), (2 * (1 - odd), i - s), (2 * odd, i + 3 * s))):
            yield pltpu.make_async_remote_copy(
                src_ref=xb.at[1, LAST, pl.ds(OWN + INNER, CH)],
                dst_ref=raw_in.at[pl.ds(pl.multiple_of(slot * CH, CH), CH)],
                send_sem=ws.at[f], recv_sem=wr.at[f],
                device_id=(to, r), device_id_type=MESH), inside(to), inside(to)

    def start(copies):
        for copy, to, _ in copies:
            @pl.when(to)
            def _():
                copy.start()

    def sent(copies):
        for copy, to, _ in copies:
            @pl.when(to)
            def _():
                copy.wait_send()

    def arrived(copies):
        for copy, _, come in copies:
            @pl.when(come)
            def _():
                copy.wait_recv()

    def receive(rnd, y):
        arrived(flows(rnd, y))
        for at, _, come in sides:
            @pl.when(inside(come))
            def _():
                unpack(rnd, y, at)

    def partial_copy(rnd, y):
        return pltpu.make_async_remote_copy(
            src_ref=part_out.at[rnd, y], dst_ref=part_in.at[rnd, y],
            send_sem=ps.at[rnd, y], recv_sem=pr.at[rnd, y],
            device_id=(pair, r), device_id_type=MESH)

    def halo(rnd, side, kind):
        src, dst, to, come = ((1, ROWS + 1, r - 1, r + 1), (ROWS, 0, r + 1, r - 1))[side]
        if kind == 0:
            ends = (mixed.at[rnd, pl.ds(src * BLOCK, INNER), :], mixed.at[rnd, pl.ds(dst * BLOCK, INNER), :])
        else:
            ends = (mixed.at[rnd, pl.ds(src * BLOCK + INNER, CH), :], side_in.at[rnd, side])
        return [(pltpu.make_async_remote_copy(
            src_ref=ends[0], dst_ref=ends[1], send_sem=hs.at[rnd, side, kind], recv_sem=hr.at[rnd, side, kind],
            device_id=(i, to), device_id_type=MESH), row_inside(to), row_inside(come))]

    loads[0].wait()
    for y in ORDER:
        for p in range(HALF):
            xb[0, y, OWN + p * CH:OWN + (p + 1) * CH, 0:WIDTH] = x_ref[pl.ds(plane_at(p), CH), y, :]
        pack(0, y)
        if y == ORDER[0]:
            pl.semaphore_wait(barrier, count)
        if y in ORDER[:FIRST]:
            start(flows(0, y))

    for rnd in range(ROUNDS):
        for y in range(ROWS):
            @pl.when(i < 2)
            def _():
                xb[rnd, y, 0:BLOCK, :] = jnp.zeros((BLOCK, LANES), jnp.bfloat16)

            @pl.when(i >= n_off - 2)
            def _():
                xb[rnd, y, 2 * BLOCK:, :] = jnp.zeros((BLOCK, LANES), jnp.bfloat16)

        @pl.when(i < 2)
        def _():
            raw_in[0:CH, :] = jnp.zeros((CH, LANES), jnp.bfloat16)

        @pl.when(i >= n_off - 2)
        def _():
            raw_in[2 * CH:, :] = jnp.zeros((CH, LANES), jnp.bfloat16)

        mixed[rnd, INNER:BLOCK, :] = jnp.zeros((CH, LANES), jnp.bfloat16)
        mixed[rnd, (ROWS + 1) * BLOCK + INNER:, :] = jnp.zeros((CH, LANES), jnp.bfloat16)

        @pl.when(r == 0)
        def _():
            mixed[rnd, 0:INNER, :] = jnp.zeros((INNER, LANES), jnp.bfloat16)

        @pl.when(r == n_rows - 1)
        def _():
            mixed[rnd, (ROWS + 1) * BLOCK:(ROWS + 1) * BLOCK + INNER, :] = jnp.zeros((INNER, LANES), jnp.bfloat16)

    row = lax.broadcasted_iota(jnp.int32, (BLOCK, BLOCK), 0)
    col = lax.broadcasted_iota(jnp.int32, (BLOCK, BLOCK), 1)
    p_out, p_in = row // CH, col // CH
    spread = (lax.broadcasted_iota(jnp.int32, (CH, BLOCK), 1) % CH
              == lax.broadcasted_iota(jnp.int32, (CH, BLOCK), 0)).astype(jnp.bfloat16)
    pick = (lax.broadcasted_iota(jnp.int32, (BLOCK, CH), 0) % CH
            == lax.broadcasted_iota(jnp.int32, (BLOCK, CH), 1))
    for load in loads[1:]:
        load.wait()
    for rnd in range(ROUNDS):
        for kind, (k_ref, b_ref) in enumerate(((ok_ref, ob_ref), (sk_ref, sb_ref))):
            bias[rnd, kind] = jnp.sum(jnp.where(pick, b_ref[rnd:rnd + 1, :], 0.0), axis=1, keepdims=True)
            wide = jnp.dot(k_ref[rnd], spread, preferred_element_type=jnp.float32)
            taps = [wide[t * CH:(t + 1) * CH] for t in range(9)]
            full = [jnp.concatenate([tap] * HALF, axis=0) for tap in taps]
            raw = jnp.zeros((CH, BLOCK), jnp.float32)
            for a in range(3):
                if kind == 0:
                    theirs = jnp.where(odd == 1, taps[3 * a], taps[3 * a + 2])
                    raw = jnp.where(p_in[:CH] == a, theirs, raw)
                    block = jnp.zeros((BLOCK, BLOCK), jnp.float32)
                    for b in range(3):
                        block = jnp.where(p_in - p_out == s * (b - 1), full[3 * a + b], block)
                    w_off[rnd, 0:BLOCK, a * BLOCK:(a + 1) * BLOCK] = block.astype(jnp.bfloat16)
                    outer = jnp.where(odd == 1, taps[3 * a + 2], taps[3 * a])
                    outer = jnp.where(p_in[:CH] == HALF - 1, outer, 0.0)
                    w_off[rnd, BLOCK:, a * BLOCK:(a + 1) * BLOCK] = outer.astype(jnp.bfloat16)
                    if rnd == 1:
                        w_raw[...] = raw.astype(jnp.bfloat16)
                else:
                    for b in range(3):
                        block = jnp.where(p_in == p_out, full[3 * a + b], 0.0)
                        w_sp[rnd, b * BLOCK:(b + 1) * BLOCK, a * BLOCK:(a + 1) * BLOCK] = block.astype(jnp.bfloat16)

    image = lax.broadcasted_iota(jnp.int32, (BLOCK, LANES), 1) < WIDTH

    def mix(rnd, y):
        sums = jnp.dot(w_off[rnd], xb[rnd, y], preferred_element_type=jnp.float32)
        if (rnd, y) != (1, LAST):
            part_out[rnd, y] = sums[BLOCK:].astype(jnp.bfloat16)
            partial_copy(rnd, y).start()
        sums = sums[:BLOCK] + bias[rnd, 0]
        held[y] = sums[INNER:]
        value = jnp.where(image, jnp.maximum(sums, 0.0), 0.0)
        mixed[rnd, (y + 1) * BLOCK:(y + 2) * BLOCK, :] = value.astype(jnp.bfloat16)
        if y in (0, ROWS - 1):
            start(halo(rnd, 0 if y == 0 else 1, 0))

    def mix_last(rnd, y):
        if (rnd, y) != (1, LAST):
            partial_copy(rnd, y).wait_recv()
            sums = held[y] + part_in[rnd, y].astype(jnp.float32)
        else:
            arrived(raw_flows())
            sums = held[y] + jnp.dot(w_raw[:, 0:3 * CH], raw_in[...], preferred_element_type=jnp.float32)
        value = jnp.where(image[:CH], jnp.maximum(sums, 0.0), 0.0)
        mixed[rnd, (y + 1) * BLOCK + INNER:(y + 2) * BLOCK, :] = value.astype(jnp.bfloat16)
        if y in (0, ROWS - 1):
            start(halo(rnd, 0 if y == 0 else 1, 1))

    def filtered(parts, biases):
        n = parts.shape[0] // 3
        sums = (pltpu.roll(parts[:n], 1, 1) + parts[n:2 * n]
                + pltpu.roll(parts[2 * n:], LANES - 1, 1) + biases)
        return jnp.maximum(sums, 0.0).astype(jnp.bfloat16)

    def spatial(rnd, y):
        parts = jnp.dot(w_sp[rnd], mixed[rnd, y * BLOCK:(y + 3) * BLOCK, :], preferred_element_type=jnp.float32)
        value = filtered(parts, bias[rnd, 1])
        if rnd == 0:
            xb[1, y, OWN:OWN + INNER, :] = value[:INNER]
            pack(1, y)
        else:
            for p in range(HALF - 1):
                o_ref[pl.ds(plane_at(p), CH), y, :] = value[p * CH:(p + 1) * CH, :WIDTH]

    def spatial_last(rnd):
        for side in range(2):
            dst = (ROWS + 1, 0)[side]

            @pl.when(row_inside((r + 1, r - 1)[side]))
            def _():
                mixed[rnd, dst * BLOCK + INNER:(dst + 1) * BLOCK, :] = side_in[rnd, side]
        weights = jnp.concatenate([w_sp[rnd, b * BLOCK + INNER:(b + 1) * BLOCK, :] for b in range(3)], axis=0)
        for y in range(ROWS):
            parts = jnp.dot(weights, mixed[rnd, y * BLOCK:(y + 3) * BLOCK, :], preferred_element_type=jnp.float32)
            value = filtered(parts, bias[rnd, 1, INNER:])
            if rnd == 0:
                xb[1, y, OWN + INNER:OWN + BLOCK, :] = value
            else:
                o_ref[pl.ds(plane_at(HALF - 1), CH), y, :] = value[:, :WIDTH]

    for rnd in range(ROUNDS):
        for n, y in enumerate(ORDER):
            receive(rnd, y)
            if rnd == 1 and n == 0:
                arrived(edge_flows())
            mix(rnd, y)
            if rnd == 0 and n + FIRST < ROWS:
                start(flows(0, ORDER[n + FIRST]))
            if n == 2:
                arrived(halo(rnd, 1, 0))
                spatial(rnd, 0)
                if rnd == 0:
                    start(flows(1, 0))
            if n == 3:
                arrived(halo(rnd, 0, 0))
                spatial(rnd, 3)
                if rnd == 0:
                    start(flows(1, 3))
                spatial(rnd, 1)
                spatial(rnd, 2)
            if n > 0:
                mix_last(rnd, ORDER[n - 1])
        mix_last(rnd, ORDER[-1])
        for side in range(2):
            arrived(halo(rnd, side, 1))
        spatial_last(rnd)
        if rnd == 0:
            start(edge_flows())
            start(raw_flows())
            start(flows(1, 1))
            start(flows(1, 2))

    sent(edge_flows())
    sent(raw_flows())
    for rnd in range(ROUNDS):
        for y in range(ROWS):
            sent(flows(rnd, y))
            if (rnd, y) != (1, LAST):
                partial_copy(rnd, y).wait_send()
        for side in range(2):
            for kind in range(2):
                sent(halo(rnd, side, kind))


def local(volume, offset_kernels, offset_biases, spatial_kernels, spatial_biases):
    n_off, n_rows = lax.axis_size("off"), lax.axis_size("rows")
    out = pl.pallas_call(
        lambda *refs: kernel(n_off, n_rows, *refs),
        out_shape=pltpu.VMEM((BLOCK, ROWS, WIDTH), jnp.bfloat16),
        in_specs=[pl.BlockSpec(memory_space=pltpu.HBM)] * 5,
        out_specs=pl.BlockSpec(memory_space=pltpu.VMEM),
        scratch_shapes=[
            pltpu.VMEM((BLOCK, ROWS, WIDTH), jnp.bfloat16),
            pltpu.VMEM((ROUNDS, 9 * CH, CH), jnp.bfloat16),
            pltpu.VMEM((ROUNDS, CH), jnp.float32),
            pltpu.VMEM((ROUNDS, 9 * CH, CH), jnp.bfloat16),
            pltpu.VMEM((ROUNDS, CH), jnp.float32),
            pltpu.SemaphoreType.DMA((5,)),
            pltpu.VMEM((ROUNDS, ROWS, 3 * BLOCK, LANES), jnp.bfloat16),
            pltpu.VMEM((ROUNDS, (ROWS + 2) * BLOCK, LANES), jnp.bfloat16),
            pltpu.VMEM((ROUNDS, ROWS, REST, BLOCK), jnp.bfloat16),
            pltpu.VMEM((ROUNDS, ROWS, CH, LANES), jnp.bfloat16),
            pltpu.VMEM((ROUNDS, ROWS, CH, LANES), jnp.bfloat16),
            pltpu.VMEM((ROWS, CH, LANES), jnp.float32),
            pltpu.VMEM((ROUNDS, 2, CH, LANES), jnp.bfloat16),
            pltpu.VMEM((3 * CH, LANES), jnp.bfloat16),
            pltpu.VMEM((ROUNDS, BLOCK + CH, 3 * BLOCK), jnp.bfloat16),
            pltpu.VMEM((ROUNDS, 3 * BLOCK, 3 * BLOCK), jnp.bfloat16),
            pltpu.VMEM((CH, BLOCK), jnp.bfloat16),
            pltpu.VMEM((ROUNDS, 2, BLOCK, 1), jnp.float32),
            pltpu.SemaphoreType.DMA((ROUNDS, ROWS, 4)),
            pltpu.SemaphoreType.DMA((ROUNDS, ROWS, 4)),
            pltpu.SemaphoreType.DMA((ROUNDS, ROWS)),
            pltpu.SemaphoreType.DMA((ROUNDS, ROWS)),
            pltpu.SemaphoreType.DMA((2,)),
            pltpu.SemaphoreType.DMA((2,)),
            pltpu.SemaphoreType.DMA((ROUNDS, 2, 2)),
            pltpu.SemaphoreType.DMA((ROUNDS, 2, 2)),
            pltpu.SemaphoreType.DMA((3,)),
            pltpu.SemaphoreType.DMA((3,)),
        ],
        compiler_params=pltpu.CompilerParams(collective_id=0, has_side_effects=True, vmem_limit_bytes=40 << 20),
        cost_estimate=pl.CostEstimate(flops=1 << 30, bytes_accessed=1 << 20, transcendentals=0),
        name="filter_rounds",
    )(*[pltpu.with_memory_space_constraint(a, pltpu.HBM) for a in (
        volume.reshape(BLOCK, ROWS, WIDTH), offset_kernels.reshape(ROUNDS, 9 * CH, CH), offset_biases,
        spatial_kernels.reshape(ROUNDS, 9 * CH, CH), spatial_biases)])
    return out.reshape(HALF, CH, ROWS, WIDTH)


def solution(mesh):
    in_specs = (P("off", None, "rows", None), P(), P(), P(), P())
    out_specs = P("off", None, "rows", None)
    return jax.shard_map(local, mesh=mesh, in_specs=in_specs, out_specs=out_specs, check_vma=False)
```

```python
import jax
import jax.numpy as jnp
from jax import lax
from jax.experimental import pallas as pl
from jax.experimental.pallas import tpu as pltpu
from jax.sharding import PartitionSpec as P

MESH = pl.DeviceIdType.MESH
CH = 16
ROUNDS = 2
HALF = 8
BLOCK = HALF * CH
INNER = BLOCK - CH
ROWS = 4
WIDTH = 480
LANES = 512
WHOLE = 384
REST = 96
QUARTER = BLOCK - REST
OWN = BLOCK
ORDER = (0, 3, 1, 2)
FIRST = 3


def kernel(n_off, n_rows, x_hbm, ok_hbm, ob_hbm, sk_hbm, sb_hbm, o_ref,
           x_ref, ok_ref, ob_ref, sk_ref, sb_ref, ls,
           xb, mixed, packed, part_out, part_in, held, side_in, w_off, w_sp, bias,
           ss, rs, ps, pr, es, er, hs, hr):
    i, r = lax.axis_index("off"), lax.axis_index("rows")
    odd = lax.rem(i, 2)
    s = 1 - 2 * odd
    pair = i + s

    def inside(t):
        return (t >= 0) & (t < n_off)

    def row_inside(t):
        return (t >= 0) & (t < n_rows)

    loads = [pltpu.make_async_copy(a, b, ls.at[n]) for n, (a, b) in enumerate(
        ((x_hbm, x_ref), (ok_hbm, ok_ref), (ob_hbm, ob_ref), (sk_hbm, sk_ref), (sb_hbm, sb_ref)))]
    for load in loads:
        load.start()

    barrier = pltpu.get_barrier_semaphore()
    count = jnp.int32(1)
    pl.semaphore_signal(barrier, inc=1, device_id=(pair, r), device_id_type=MESH)
    for t in (i - 2, i + 2):
        @pl.when(inside(t))
        def _():
            pl.semaphore_signal(barrier, inc=1, device_id=(t, r), device_id_type=MESH)
        count = count + inside(t).astype(jnp.int32)
    for t in (r - 1, r + 1):
        @pl.when(row_inside(t))
        def _():
            pl.semaphore_signal(barrier, inc=1, device_id=(i, t), device_id_type=MESH)
        count = count + row_inside(t).astype(jnp.int32)

    def plane_at(p):
        return pl.multiple_of(CH * (p + odd * (HALF - 1 - 2 * p)), CH)

    lane = lax.broadcasted_iota(jnp.int32, (QUARTER, BLOCK), 1)

    def pack(rnd, y):
        n = QUARTER if rnd == 0 else CH
        last = xb[rnd, y, OWN + REST:OWN + REST + n, WHOLE:].astype(jnp.float32)
        for g in range(3):
            at = g * QUARTER
            keep = xb[rnd, y, OWN + at:OWN + at + n, WHOLE:]
            moved = pltpu.roll(last, REST - at, 1).astype(jnp.bfloat16)
            packed[rnd, y, at:at + n, :] = jnp.where(lane[:n] < REST, keep, moved)
            if n < QUARTER:
                packed[rnd, y, at + n:at + QUARTER, :] = xb[rnd, y, OWN + at + n:OWN + at + QUARTER, WHOLE:]

    def unpack(rnd, y, base):
        n = QUARTER if rnd == 0 else CH
        value = None
        for g in (2, 1, 0):
            at = base + g * QUARTER
            moved = pltpu.roll(xb[rnd, y, at:at + n, WHOLE:].astype(jnp.float32), (g + 1) * QUARTER, 1)
            value = moved if value is None else jnp.where(lane[:n] < (g + 1) * QUARTER, moved, value)
        xb[rnd, y, base + REST:base + REST + n, WHOLE:] = value.astype(jnp.bfloat16)

    sides = ((0, i + 2, i - 2), (2 * BLOCK, i - 2, i + 2))

    def flows(rnd, y):
        n = BLOCK if rnd == 0 else INNER
        for f, (at, to, come) in enumerate(sides):
            yield pltpu.make_async_remote_copy(
                src_ref=packed.at[rnd, y],
                dst_ref=xb.at[rnd, y, pl.ds(at, REST), pl.ds(WHOLE, BLOCK)],
                send_sem=ss.at[rnd, y, 2 * f + 1], recv_sem=rs.at[rnd, y, 2 * f + 1],
                device_id=(to, r), device_id_type=MESH), inside(to), inside(come)
            yield pltpu.make_async_remote_copy(
                src_ref=xb.at[rnd, y, pl.ds(OWN, n), pl.ds(0, WHOLE)],
                dst_ref=xb.at[rnd, y, pl.ds(at, n), pl.ds(0, WHOLE)],
                send_sem=ss.at[rnd, y, 2 * f], recv_sem=rs.at[rnd, y, 2 * f],
                device_id=(to, r), device_id_type=MESH), inside(to), inside(come)

    def edge_flows():
        for f, (at, to, come) in enumerate(sides):
            yield pltpu.make_async_remote_copy(
                src_ref=xb.at[1, :, pl.ds(OWN + INNER, CH)],
                dst_ref=xb.at[1, :, pl.ds(at + INNER, CH)],
                send_sem=es.at[f], recv_sem=er.at[f],
                device_id=(to, r), device_id_type=MESH), inside(to), inside(come)

    def start(copies):
        for copy, to, _ in copies:
            @pl.when(to)
            def _():
                copy.start()

    def sent(copies):
        for copy, to, _ in copies:
            @pl.when(to)
            def _():
                copy.wait_send()

    def arrived(copies):
        for copy, _, come in copies:
            @pl.when(come)
            def _():
                copy.wait_recv()

    def receive(rnd, y):
        arrived(flows(rnd, y))
        for at, _, come in sides:
            @pl.when(inside(come))
            def _():
                unpack(rnd, y, at)

    def partial_copy(rnd, y):
        return pltpu.make_async_remote_copy(
            src_ref=part_out.at[rnd, y], dst_ref=part_in.at[rnd, y],
            send_sem=ps.at[rnd, y], recv_sem=pr.at[rnd, y],
            device_id=(pair, r), device_id_type=MESH)

    def halo(rnd, side, kind):
        src, dst, to, come = ((1, ROWS + 1, r - 1, r + 1), (ROWS, 0, r + 1, r - 1))[side]
        if kind == 0:
            ends = (mixed.at[rnd, pl.ds(src * BLOCK, INNER), :], mixed.at[rnd, pl.ds(dst * BLOCK, INNER), :])
        else:
            ends = (mixed.at[rnd, pl.ds(src * BLOCK + INNER, CH), :], side_in.at[rnd, side])
        return [(pltpu.make_async_remote_copy(
            src_ref=ends[0], dst_ref=ends[1], send_sem=hs.at[rnd, side, kind], recv_sem=hr.at[rnd, side, kind],
            device_id=(i, to), device_id_type=MESH), row_inside(to), row_inside(come))]

    loads[0].wait()
    for y in ORDER:
        for p in range(HALF):
            xb[0, y, OWN + p * CH:OWN + (p + 1) * CH, 0:WIDTH] = x_ref[pl.ds(plane_at(p), CH), y, :]
        pack(0, y)
        if y == ORDER[0]:
            pl.semaphore_wait(barrier, count)
        if y in ORDER[:FIRST]:
            start(flows(0, y))

    for rnd in range(ROUNDS):
        for y in range(ROWS):
            @pl.when(i < 2)
            def _():
                xb[rnd, y, 0:BLOCK, :] = jnp.zeros((BLOCK, LANES), jnp.bfloat16)

            @pl.when(i >= n_off - 2)
            def _():
                xb[rnd, y, 2 * BLOCK:, :] = jnp.zeros((BLOCK, LANES), jnp.bfloat16)

        mixed[rnd, INNER:BLOCK, :] = jnp.zeros((CH, LANES), jnp.bfloat16)
        mixed[rnd, (ROWS + 1) * BLOCK + INNER:, :] = jnp.zeros((CH, LANES), jnp.bfloat16)

        @pl.when(r == 0)
        def _():
            mixed[rnd, 0:INNER, :] = jnp.zeros((INNER, LANES), jnp.bfloat16)

        @pl.when(r == n_rows - 1)
        def _():
            mixed[rnd, (ROWS + 1) * BLOCK:(ROWS + 1) * BLOCK + INNER, :] = jnp.zeros((INNER, LANES), jnp.bfloat16)

    row = lax.broadcasted_iota(jnp.int32, (BLOCK, BLOCK), 0)
    col = lax.broadcasted_iota(jnp.int32, (BLOCK, BLOCK), 1)
    p_out, p_in = row // CH, col // CH
    spread = (lax.broadcasted_iota(jnp.int32, (CH, BLOCK), 1) % CH
              == lax.broadcasted_iota(jnp.int32, (CH, BLOCK), 0)).astype(jnp.bfloat16)
    pick = (lax.broadcasted_iota(jnp.int32, (BLOCK, CH), 0) % CH
            == lax.broadcasted_iota(jnp.int32, (BLOCK, CH), 1))
    for load in loads[1:]:
        load.wait()
    for rnd in range(ROUNDS):
        for kind, (k_ref, b_ref) in enumerate(((ok_ref, ob_ref), (sk_ref, sb_ref))):
            bias[rnd, kind] = jnp.sum(jnp.where(pick, b_ref[rnd:rnd + 1, :], 0.0), axis=1, keepdims=True)
            wide = jnp.dot(k_ref[rnd], spread, preferred_element_type=jnp.float32)
            taps = [wide[t * CH:(t + 1) * CH] for t in range(9)]
            full = [jnp.concatenate([tap] * HALF, axis=0) for tap in taps]
            for a in range(3):
                if kind == 0:
                    block = jnp.zeros((BLOCK, BLOCK), jnp.float32)
                    for b in range(3):
                        block = jnp.where(p_in - p_out == s * (b - 1), full[3 * a + b], block)
                    w_off[rnd, 0:BLOCK, a * BLOCK:(a + 1) * BLOCK] = block.astype(jnp.bfloat16)
                    outer = jnp.where(odd == 1, taps[3 * a + 2], taps[3 * a])
                    outer = jnp.where(p_in[:CH] == HALF - 1, outer, 0.0)
                    w_off[rnd, BLOCK:, a * BLOCK:(a + 1) * BLOCK] = outer.astype(jnp.bfloat16)
                else:
                    for b in range(3):
                        block = jnp.where(p_in == p_out, full[3 * a + b], 0.0)
                        w_sp[rnd, b * BLOCK:(b + 1) * BLOCK, a * BLOCK:(a + 1) * BLOCK] = block.astype(jnp.bfloat16)

    image = lax.broadcasted_iota(jnp.int32, (BLOCK, LANES), 1) < WIDTH

    def mix(rnd, y):
        sums = jnp.dot(w_off[rnd], xb[rnd, y], preferred_element_type=jnp.float32)
        part_out[rnd, y] = sums[BLOCK:].astype(jnp.bfloat16)
        partial_copy(rnd, y).start()
        sums = sums[:BLOCK] + bias[rnd, 0]
        held[y] = sums[INNER:]
        value = jnp.where(image, jnp.maximum(sums, 0.0), 0.0)
        mixed[rnd, (y + 1) * BLOCK:(y + 2) * BLOCK, :] = value.astype(jnp.bfloat16)
        if y in (0, ROWS - 1):
            start(halo(rnd, 0 if y == 0 else 1, 0))

    def mix_last(rnd, y):
        partial_copy(rnd, y).wait_recv()
        sums = held[y] + part_in[rnd, y].astype(jnp.float32)
        value = jnp.where(image[:CH], jnp.maximum(sums, 0.0), 0.0)
        mixed[rnd, (y + 1) * BLOCK + INNER:(y + 2) * BLOCK, :] = value.astype(jnp.bfloat16)
        if y in (0, ROWS - 1):
            start(halo(rnd, 0 if y == 0 else 1, 1))

    def filtered(parts, biases):
        n = parts.shape[0] // 3
        sums = (pltpu.roll(parts[:n], 1, 1) + parts[n:2 * n]
                + pltpu.roll(parts[2 * n:], LANES - 1, 1) + biases)
        return jnp.maximum(sums, 0.0).astype(jnp.bfloat16)

    def spatial(rnd, y):
        parts = jnp.dot(w_sp[rnd], mixed[rnd, y * BLOCK:(y + 3) * BLOCK, :], preferred_element_type=jnp.float32)
        value = filtered(parts, bias[rnd, 1])
        if rnd == 0:
            xb[1, y, OWN:OWN + INNER, :] = value[:INNER]
            pack(1, y)
        else:
            for p in range(HALF - 1):
                o_ref[pl.ds(plane_at(p), CH), y, :] = value[p * CH:(p + 1) * CH, :WIDTH]

    def spatial_last(rnd):
        for side in range(2):
            dst = (ROWS + 1, 0)[side]

            @pl.when(row_inside((r + 1, r - 1)[side]))
            def _():
                mixed[rnd, dst * BLOCK + INNER:(dst + 1) * BLOCK, :] = side_in[rnd, side]
        weights = jnp.concatenate([w_sp[rnd, b * BLOCK + INNER:(b + 1) * BLOCK, :] for b in range(3)], axis=0)
        for y in range(ROWS):
            parts = jnp.dot(weights, mixed[rnd, y * BLOCK:(y + 3) * BLOCK, :], preferred_element_type=jnp.float32)
            value = filtered(parts, bias[rnd, 1, INNER:])
            if rnd == 0:
                xb[1, y, OWN + INNER:OWN + BLOCK, :] = value
            else:
                o_ref[pl.ds(plane_at(HALF - 1), CH), y, :] = value[:, :WIDTH]

    for rnd in range(ROUNDS):
        for n, y in enumerate(ORDER):
            receive(rnd, y)
            if rnd == 1 and n == 0:
                arrived(edge_flows())
            mix(rnd, y)
            if rnd == 0 and n + FIRST < ROWS:
                start(flows(0, ORDER[n + FIRST]))
            if n == 2:
                arrived(halo(rnd, 1, 0))
                spatial(rnd, 0)
                if rnd == 0:
                    start(flows(1, 0))
            if n == 3:
                arrived(halo(rnd, 0, 0))
                spatial(rnd, 3)
                if rnd == 0:
                    start(flows(1, 3))
                spatial(rnd, 1)
                spatial(rnd, 2)
            if n > 0:
                mix_last(rnd, ORDER[n - 1])
        mix_last(rnd, ORDER[-1])
        for side in range(2):
            arrived(halo(rnd, side, 1))
        spatial_last(rnd)
        if rnd == 0:
            start(edge_flows())
            start(flows(1, 1))
            start(flows(1, 2))

    sent(edge_flows())
    for rnd in range(ROUNDS):
        for y in range(ROWS):
            sent(flows(rnd, y))
            partial_copy(rnd, y).wait_send()
        for side in range(2):
            for kind in range(2):
                sent(halo(rnd, side, kind))


def local(volume, offset_kernels, offset_biases, spatial_kernels, spatial_biases):
    n_off, n_rows = lax.axis_size("off"), lax.axis_size("rows")
    out = pl.pallas_call(
        lambda *refs: kernel(n_off, n_rows, *refs),
        out_shape=pltpu.VMEM((BLOCK, ROWS, WIDTH), jnp.bfloat16),
        in_specs=[pl.BlockSpec(memory_space=pltpu.HBM)] * 5,
        out_specs=pl.BlockSpec(memory_space=pltpu.VMEM),
        scratch_shapes=[
            pltpu.VMEM((BLOCK, ROWS, WIDTH), jnp.bfloat16),
            pltpu.VMEM((ROUNDS, 9 * CH, CH), jnp.bfloat16),
            pltpu.VMEM((ROUNDS, CH), jnp.float32),
            pltpu.VMEM((ROUNDS, 9 * CH, CH), jnp.bfloat16),
            pltpu.VMEM((ROUNDS, CH), jnp.float32),
            pltpu.SemaphoreType.DMA((5,)),
            pltpu.VMEM((ROUNDS, ROWS, 3 * BLOCK, LANES), jnp.bfloat16),
            pltpu.VMEM((ROUNDS, (ROWS + 2) * BLOCK, LANES), jnp.bfloat16),
            pltpu.VMEM((ROUNDS, ROWS, REST, BLOCK), jnp.bfloat16),
            pltpu.VMEM((ROUNDS, ROWS, CH, LANES), jnp.bfloat16),
            pltpu.VMEM((ROUNDS, ROWS, CH, LANES), jnp.bfloat16),
            pltpu.VMEM((ROWS, CH, LANES), jnp.float32),
            pltpu.VMEM((ROUNDS, 2, CH, LANES), jnp.bfloat16),
            pltpu.VMEM((ROUNDS, BLOCK + CH, 3 * BLOCK), jnp.bfloat16),
            pltpu.VMEM((ROUNDS, 3 * BLOCK, 3 * BLOCK), jnp.bfloat16),
            pltpu.VMEM((ROUNDS, 2, BLOCK, 1), jnp.float32),
            pltpu.SemaphoreType.DMA((ROUNDS, ROWS, 4)),
            pltpu.SemaphoreType.DMA((ROUNDS, ROWS, 4)),
            pltpu.SemaphoreType.DMA((ROUNDS, ROWS)),
            pltpu.SemaphoreType.DMA((ROUNDS, ROWS)),
            pltpu.SemaphoreType.DMA((2,)),
            pltpu.SemaphoreType.DMA((2,)),
            pltpu.SemaphoreType.DMA((ROUNDS, 2, 2)),
            pltpu.SemaphoreType.DMA((ROUNDS, 2, 2)),
        ],
        compiler_params=pltpu.CompilerParams(collective_id=0, has_side_effects=True, vmem_limit_bytes=40 << 20),
        cost_estimate=pl.CostEstimate(flops=1 << 30, bytes_accessed=1 << 20, transcendentals=0),
        name="filter_rounds",
    )(*[pltpu.with_memory_space_constraint(a, pltpu.HBM) for a in (
        volume.reshape(BLOCK, ROWS, WIDTH), offset_kernels.reshape(ROUNDS, 9 * CH, CH), offset_biases,
        spatial_kernels.reshape(ROUNDS, 9 * CH, CH), spatial_biases)])
    return out.reshape(HALF, CH, ROWS, WIDTH)


def solution(mesh):
    in_specs = (P("off", None, "rows", None), P(), P(), P(), P())
    out_specs = P("off", None, "rows", None)
    return jax.shard_map(local, mesh=mesh, in_specs=in_specs, out_specs=out_specs, check_vma=False)
```
